32 devices in a mesh: parts: 2 (over x), tile: 16 (over z, y, core).
Axes of the slice: x: 2, y: 2, z: 4, core: 2. Of those that a mesh axis runs over, the one named last changes fastest.
Arguments:
- features: bfloat16 [512, 2560, 128], P(('parts', 'tile')), parts along dimension 0, may hold values from -40 to 40
- links: int32 [512, 2560], P(('parts', 'tile')), parts along dimension 0, may hold values from 0 to 511, as said below
- coarse_links: int32 [128, 640], P(('parts', 'tile')), parts along dimension 0, may hold values from 0 to 511, as said below
- fine_weight: bfloat16 [5, 128, 128], replicated, may hold values from -0.25693506 to 0.25693506
- fine_bias: float32 [128], replicated, may hold values from -1.5 to 1.5
- coarse_weight: bfloat16 [5, 128, 128], replicated, may hold values from -0.25693506 to 0.25693506
- coarse_bias: float32 [128], replicated, may hold values from -1.5 to 1.5
Outputs:
- fine_map: bfloat16 [512, 2560, 128], P(('parts', 'tile')), parts along dimension 0
- coarse_map: bfloat16 [128, 640, 128], P(('parts', 'tile')), parts along dimension 0
- pooled: float32 [256], P('parts'), parts along dimension 0
The draws below stay inside these ranges and needn't reach their ends.
There are 2 independent parts, one for each index of `parts`. The reference program is written for one: setup_inputs(seed, part) draws one part's arguments, and reference() takes and returns one part's arrays. A program takes and returns all parts, laid end to end along the dimension named above; an argument that names none is the same for every part. Nothing has to cross between parts.
Inputs may be any that keep to these rules, and one draw needn't show every extreme that they name: Bits 0..7 of a code mark links to the neighbours in the eight directions of the steps, bit 8 marks a real pixel; higher bits are 0. In every row the real pixels are a leading run of at least 1280 slots (of the pooled map, at least 320), followed by padding in every row. Links join only real pixels within the grid, and a link is set where both pixels are real except that some pixels lack one diagonal link. `coarse_links`: the same rules as for links, on the pooled grid; a pooled pixel is real exactly where the full-resolution pixel at its block's first row and slot is real.
All inputs are finite; a program needn't handle non-finite values.
Results may differ from the reference program's by a relative error of at most 0.017.
Values may be sent and summed in bfloat16 or wider, within the bound.
A program may use at most 256 MiB of HBM per device.

```python
import math
import jax
import jax.numpy as jnp
from jax import lax

C = 128
ORDER = 4
COLS = 2560
ROWS = 256


link_steps = ((-1, 0), (1, 0), (0, -1), (0, 1), (-1, -1), (-1, 1), (1, -1), (1, 1))


def shape_tables(key):
    row_lengths = jax.random.randint(jax.random.fold_in(key, 11), (ROWS, 1), COLS // 2, COLS - 3)
    fine_cut = jax.random.randint(jax.random.fold_in(key, 12), (ROWS, COLS), 0, 64)
    coarse_cut = jax.random.randint(jax.random.fold_in(key, 13), (ROWS // 4, COLS // 4), 0, 64)
    columns = lax.broadcasted_iota(jnp.int32, (ROWS, COLS), 1)
    fine_real = (columns < row_lengths).astype(jnp.int32)
    return (fine_real, fine_cut, coarse_cut)


def code_table(real_grid, cut_grid):
    row_count, col_count = real_grid.shape
    padded = jnp.pad(real_grid, 1)
    link_codes = real_grid * 256
    for bit_index, (row_step, col_step) in enumerate(link_steps):
        neighbour = padded[1 + row_step:1 + row_step + row_count, 1 + col_step:1 + col_step + col_count]
        linked = real_grid * neighbour
        if bit_index >= 4:
            linked = linked * (cut_grid != bit_index - 4).astype(jnp.int32)
        link_codes = link_codes + linked * 2 ** bit_index
    return link_codes.astype(jnp.int32)


def draw_links(key, part):
    fine_real, fine_cut, coarse_cut = shape_tables(key)
    return code_table(fine_real, fine_cut)


def draw_coarse_links(key, part):
    fine_real, fine_cut, coarse_cut = shape_tables(key)
    return code_table(fine_real[::4, ::4], coarse_cut)


def row_offsets(key, strength):
    signs = jnp.where(jax.random.bernoulli(jax.random.fold_in(key, 4), 0.5, (ROWS, 1, C)), 1.0, -1.0)
    sizes = jax.random.uniform(jax.random.fold_in(key, 5), (ROWS, 1, C), jnp.float32, 0.75, 1.25)
    return strength * signs * sizes


def draw_features(key, part):
    key = jax.random.fold_in(key, 3)
    rows_up = lax.broadcasted_iota(jnp.float32, (ROWS, 1, 1), 0) / (ROWS - 1)
    row_scale = 0.2 * jnp.power(10.0, rows_up)
    channel_scale = jnp.exp(jax.random.uniform(jax.random.fold_in(key, 1), (1, 1, C), jnp.float32, -1.15, 1.15))
    values = jnp.clip(jax.random.normal(jax.random.fold_in(key, 2), (ROWS, COLS, C), jnp.float32), -3.0, 3.0)
    values = values + row_offsets(key, 2.5)
    return (values * row_scale * channel_scale).astype(jnp.bfloat16)


def chebyshev_weight(key):
    order_index = lax.broadcasted_iota(jnp.int32, (ORDER + 1, 1, 1), 0)
    gains = jnp.where(order_index == ORDER, 2.0, 0.5)
    values = jnp.clip(jax.random.normal(key, (ORDER + 1, C, C), jnp.float32), -3.0, 3.0)
    return (values * gains / math.sqrt(C * (ORDER + 1))).astype(jnp.bfloat16)


def draw_fine_weight(key, part):
    key = jax.random.fold_in(key, 21)
    return chebyshev_weight(key)


def draw_coarse_weight(key, part):
    key = jax.random.fold_in(key, 22)
    return chebyshev_weight(key)


def centred(rng, extent, spread, limit, kind=jnp.bfloat16):
    return jnp.clip(spread * jax.random.normal(rng, extent, jnp.float32), -limit, limit).astype(kind)


def setup_inputs(seed: int = 0, part: int = 0) -> dict:
    streams_of = jax.random.split(jax.random.key(seed), 8)
    own_keys = jax.random.split(jax.random.fold_in(streams_of[7], part), 8)
    return {
        "features": draw_features(jax.random.fold_in(jax.random.fold_in(streams_of[7], part), 71), part),
        "links": draw_links(jax.random.fold_in(jax.random.fold_in(streams_of[7], part), 71), part),
        "coarse_links": draw_coarse_links(jax.random.fold_in(jax.random.fold_in(streams_of[7], part), 71), part),
        "fine_weight": draw_fine_weight(jax.random.fold_in(streams_of[7], 71), part),
        "fine_bias": centred(streams_of[4], (C,), 0.25, 1.5, jnp.float32),
        "coarse_weight": draw_coarse_weight(jax.random.fold_in(streams_of[7], 71), part),
        "coarse_bias": centred(streams_of[6], (C,), 0.25, 1.5, jnp.float32),
    }


link_steps = ((-1, 0), (1, 0), (0, -1), (0, 1), (-1, -1), (-1, 1), (1, -1), (1, 1))


def neighbour_mean(padded, link_codes, row_count):
    col_count = link_codes.shape[1]
    wide_rows = jnp.pad(padded, ((0, 0), (1, 1), (0, 0)))
    running = jnp.zeros((row_count, col_count, padded.shape[2]), jnp.float32)
    degree = jnp.zeros((row_count, col_count), jnp.float32)
    for bit_index, (row_step, col_step) in enumerate(link_steps):
        link_flag = ((link_codes >> bit_index) & 1).astype(jnp.float32)
        shifted = wide_rows[1 + row_step:1 + row_step + row_count, 1 + col_step:1 + col_step + col_count]
        running = running + link_flag[:, :, None] * shifted.astype(jnp.float32)
        degree = degree + link_flag
    return -running / jnp.maximum(degree, 1.0)[:, :, None]


def project(term_rows, weight_slab):
    flattened = term_rows.reshape(-1, term_rows.shape[-1])
    product = jnp.dot(flattened, weight_slab, preferred_element_type=jnp.float32)
    return product.reshape(term_rows.shape[:-1] + (weight_slab.shape[1],))


def real_of(link_codes):
    return ((link_codes >> 8) & 1).astype(jnp.float32)[:, :, None]


def layer_output(mixed_sum, bias_row, real_mask):
    return (real_mask * jax.nn.relu(mixed_sum + bias_row)).astype(jnp.bfloat16)


def chebyshev_layer(field_in, link_codes, weights, bias_row, extend):
    row_count = field_in.shape[0]
    real_mask = real_of(link_codes)
    mixed_sum = project(field_in, weights[0])
    current = field_in
    previous = field_in
    for order_index in range(1, weights.shape[0]):
        image_term = neighbour_mean(extend(current), link_codes, row_count)
        if order_index == 1:
            fresh_term = real_mask * image_term
        else:
            fresh_term = real_mask * (2.0 * image_term - previous.astype(jnp.float32))
        fresh_term = fresh_term.astype(jnp.bfloat16)
        mixed_sum = mixed_sum + project(fresh_term, weights[order_index])
        previous, current = current, fresh_term
    return layer_output(mixed_sum, bias_row, real_mask)


def pool_pairs(grid):
    row_count, col_count, width_count = grid.shape
    blocks = grid.astype(jnp.float32).reshape(row_count // 2, 2, col_count // 2, 2, width_count)
    return jnp.mean(blocks, axis=(1, 3)).astype(jnp.bfloat16)


def zero_rim(values):
    return jnp.pad(values, ((1, 1), (0, 0), (0, 0)))


def reference(features, links, coarse_links, fine_weight, fine_bias, coarse_weight, coarse_bias):
    fine_map = chebyshev_layer(features, links, fine_weight, fine_bias, zero_rim)
    coarse_in = pool_pairs(pool_pairs(fine_map))
    coarse_map = chebyshev_layer(coarse_in, coarse_links, coarse_weight, coarse_bias, zero_rim)
    column_sums = jnp.sum(coarse_map.astype(jnp.float32), axis=(0, 1))
    real_count = jnp.sum(((coarse_links >> 8) & 1).astype(jnp.float32))
    pooled = column_sums / real_count
    return fine_map, coarse_map, pooled
```

```python
import jax
import jax.numpy as jnp
import numpy as np
from jax import lax
from jax.experimental import pallas as pl
from jax.experimental.pallas import tpu as pltpu
from jax.sharding import PartitionSpec as P

USE = 64
WIN = 80
EDGE = 16
DEEP = 4
link_steps = ((-1, 0), (1, 0), (0, -1), (0, 1), (-1, -1), (-1, 1), (1, -1), (1, 1))


def bit_table():
    table = np.zeros((WIN, 256), np.int32)
    for bit, (dr, dc) in enumerate(link_steps):
        for i in range(WIN):
            table[i, (dr + 1) * WIN + (i + dc) % WIN] = 1 << bit
    return table


def pool_tables():
    first = np.zeros((64, 256), np.float32)
    for row in range(2):
        for col in range(32):
            for dr in range(2):
                for dc in range(2):
                    first[row * 32 + col, (2 * row + dr) * 64 + 2 * col + dc] = 0.25
    second = np.zeros((16, 64), np.float32)
    for col in range(16):
        for dr in range(2):
            for dc in range(2):
                second[col, dr * 32 + 2 * col + dc] = 0.25
    return first, second


def window_kernel(rows, pool, refs):
    (main, left, right, tmain, tleft, tright, bmain, bleft, bright, codes, bits, w01, w23, w4, bias) = refs[:15]
    rest = refs[15:]
    if pool:
        pool1, pool2, _, out, coarse = rest[:5]
        rest = rest[5:]
    else:
        out, sums = rest[:2]
        rest = rest[2:]
    p0, p1, p2, p3, p4, links, coef = rest
    step = pl.program_id(0)
    full = rows + 2 * DEEP

    @pl.when(step == 0)
    def _():
        for ref in (p0, p1, p2, p3, p4):
            ref[...] = jnp.zeros_like(ref)
        if not pool:
            sums[...] = jnp.zeros_like(sums)

    code = codes[0]
    degree = jnp.zeros(code.shape, jnp.int32)
    for bit in range(8):
        degree = degree + ((code >> bit) & 1)
    scale = -2.0 / jnp.maximum(degree.astype(jnp.float32), 1.0)
    real = ((code >> 8) & 1).astype(jnp.float32)
    table = bits[...]
    low = lax.broadcasted_iota(jnp.int32, (EDGE, 128), 0) < 8

    for r in range(full):
        if r < DEEP:
            m, a, b, s = tmain, tleft, tright, r
        elif r < DEEP + rows:
            m, a, b, s = main, left, right, r - DEEP
        else:
            m, a, b, s = bmain, bleft, bright, r - DEEP - rows
        mask = jnp.broadcast_to(real[:, r : r + 1], (WIN, 128))
        side = jnp.where(low, b[s].astype(jnp.float32), a[s].astype(jnp.float32))
        p0[pl.ds(r * WIN, USE), :] = (m[s].astype(jnp.float32) * mask[:USE]).astype(jnp.bfloat16)
        p0[pl.ds(r * WIN + USE, EDGE), :] = (side * mask[USE:]).astype(jnp.bfloat16)
        if 1 <= r < full - 1:
            wide = jnp.broadcast_to(code[:, r : r + 1], (WIN, 256))
            links[r] = jnp.where((wide & table) != 0, 1.0, 0.0).astype(jnp.bfloat16)
            coef[r] = jnp.broadcast_to(scale[:, r : r + 1], (WIN, 128))

    terms = (p0, p1, p2, p3, p4)
    for k in range(1, 5):
        src, dst = terms[k - 1], terms[k]
        for r in range(k, full - k):
            acc = jnp.dot(links[r], src[pl.ds((r - 1) * WIN, 256), :], preferred_element_type=jnp.float32)
            if k == 1:
                fresh = acc * (0.5 * coef[r])
            else:
                fresh = acc * coef[r] - terms[k - 2][pl.ds(r * WIN, WIN), :].astype(jnp.float32)
            dst[pl.ds(r * WIN, WIN), :] = fresh.astype(jnp.bfloat16)

    def gather(ref, first, count):
        return jnp.concatenate([ref[pl.ds((first + j) * WIN, USE), :] for j in range(count)], axis=0)

    group = 4
    for g in range(rows // group):
        first = DEEP + g * group
        q = [gather(t, first, group) for t in terms]
        mixed = jnp.dot(jnp.concatenate([q[0], q[1]], axis=1), w01[...], preferred_element_type=jnp.float32)
        mixed += jnp.dot(jnp.concatenate([q[2], q[3]], axis=1), w23[...], preferred_element_type=jnp.float32)
        mixed += jnp.dot(q[4], w4[...], preferred_element_type=jnp.float32)
        mask = jnp.concatenate(
            [jnp.broadcast_to(real[:USE, first + j : first + j + 1], (USE, 128)) for j in range(group)], axis=0
        )
        res = (mask * jnp.maximum(mixed + bias[...], 0.0)).astype(jnp.bfloat16)
        for j in range(group):
            out[g * group + j] = res[j * USE : (j + 1) * USE]
        if pool:
            half = jnp.dot(pool1[...], res, preferred_element_type=jnp.float32).astype(jnp.bfloat16)
            coarse[g] = jnp.dot(pool2[...], half, preferred_element_type=jnp.float32).astype(jnp.bfloat16)
        else:
            sums[...] += jnp.sum(res.astype(jnp.float32).reshape(-1, 8, 128), axis=0)


def layer(name, main, top, bottom, codes, weights, bias, first, count, pool, canvas=None):
    rows, cols, width = main.shape
    total = cols // USE
    chunked = top.shape[1] != cols
    ratio = USE // EDGE

    def spec(n, pick, size):
        return pl.BlockSpec((n, size, width), lambda w: (0, pick(w), 0))

    def left_of(w):
        return jnp.maximum((first + w) * ratio - 1, 0)

    def right_of(w):
        return jnp.minimum((first + w) * ratio + ratio, total * ratio - 1)

    if chunked:
        halo = [
            spec(DEEP, lambda w: w, USE),
            spec(DEEP, lambda w: jnp.where(w == 0, count * ratio + 1, w * ratio - 1), EDGE),
            spec(DEEP, lambda w: w * ratio + ratio, EDGE),
        ]
    else:
        halo = [spec(DEEP, lambda w: first + w, USE), spec(DEEP, left_of, EDGE), spec(DEEP, right_of, EDGE)]

    def whole(*shape):
        return pl.BlockSpec(shape, lambda w: (0,) * len(shape))

    full = rows + 2 * DEEP
    in_specs = (
        [spec(rows, lambda w: first + w, USE), spec(rows, left_of, EDGE), spec(rows, right_of, EDGE)]
        + halo + halo
        + [pl.BlockSpec((1, WIN, full), lambda w: (first + w, 0, 0))]
        + [whole(WIN, 256), whole(256, 128), whole(256, 128), whole(128, 128), whole(1, 128)]
    )
    operands = [main] * 3 + [top] * 3 + [bottom] * 3 + [codes, jnp.asarray(bit_table())]
    operands += [weights[0:2].reshape(256, 128), weights[2:4].reshape(256, 128), weights[4], bias.reshape(1, 128)]
    out_map = jax.ShapeDtypeStruct((rows, cols, width), jnp.bfloat16)
    aliases = {}
    if pool:
        pool1, pool2 = pool_tables()
        operands += [jnp.asarray(pool1, jnp.bfloat16), jnp.asarray(pool2, jnp.bfloat16)]
        in_specs += [whole(64, 256), whole(16, 64)]
        if canvas is None:
            operands.append(bias.reshape(1, 128))
            in_specs.append(whole(1, 128))
        else:
            aliases = {len(operands): 0}
            operands.append(canvas)
            in_specs.append(pl.BlockSpec(memory_space=pl.ANY))
        out_shape = [out_map, jax.ShapeDtypeStruct((rows // 4, count * USE // 4, width), jnp.bfloat16)]
        out_specs = [spec(rows, lambda w: first + w, USE), spec(rows // 4, lambda w: w, USE // 4)]
    else:
        out_shape = [out_map, jax.ShapeDtypeStruct((8, 128), jnp.float32)]
        out_specs = [spec(rows, lambda w: first + w, USE), whole(8, 128)]
    field = pltpu.VMEM((full * WIN + 16, 128), jnp.bfloat16)
    pixels = full * WIN * count
    return pl.pallas_call(
        lambda *refs: window_kernel(rows, pool, refs),
        grid=(count,),
        in_specs=in_specs,
        out_specs=out_specs,
        out_shape=out_shape,
        input_output_aliases=aliases,
        scratch_shapes=[field] * 5
        + [pltpu.VMEM((full, WIN, 256), jnp.bfloat16), pltpu.VMEM((full, WIN, 128), jnp.float32)],
        compiler_params=pltpu.CompilerParams(vmem_limit_bytes=40 * 2**20),
        cost_estimate=pl.CostEstimate(
            flops=pixels * 128 * 2 * 256 * 4, bytes_accessed=pixels * 128 * 4, transcendentals=0
        ),
        name=name,
    )(*operands)


def shifts():
    size = lax.axis_size("tile")
    up = [(i, i + 1) for i in range(size - 1)]
    down = [(i + 1, i) for i in range(size - 1)]
    return up, down


def code_windows(links):
    up, down = shifts()
    above = lax.ppermute(links[-DEEP:], "tile", up)
    below = lax.ppermute(links[:DEEP], "tile", down)
    codes = jnp.concatenate([above, links, below], axis=0)
    rows, cols = codes.shape
    count = cols // USE
    body = codes.reshape(rows, count, USE)
    after = jnp.pad(codes[:, USE:], ((0, 0), (0, USE))).reshape(rows, count, USE)[:, :, :8]
    before = jnp.pad(codes[:, :-USE], ((0, 0), (USE, 0))).reshape(rows, count, USE)[:, :, USE - 8 :]
    return jnp.concatenate([body, after, before], axis=2).transpose(1, 2, 0)


CHUNKS = (0.1, 0.3, 0.6, 1.0)


def on_device(features, links, coarse_links, fine_weight, fine_bias, coarse_weight, coarse_bias):
    up, down = shifts()
    rows, cols, width = features.shape
    total = cols // USE
    ends = [round(total * f) for f in CHUNKS]
    starts = [0] + ends[:-1]
    fine_codes = code_windows(links)
    coarse_codes = code_windows(coarse_links)
    halos = []
    for lo, hi in zip(starts, ends):
        a, b = lo * USE, hi * USE
        right = min(b, cols - EDGE)
        left = max(a - EDGE, 0)

        def piece(part):
            return jnp.concatenate(
                [part[:, a:b], part[:, right : right + EDGE], part[:, left : left + EDGE]], axis=1
            )

        above = lax.ppermute(piece(features[-DEEP:]), "tile", up)
        below = lax.ppermute(piece(features[:DEEP]), "tile", down)
        halos.append((above, below))
    canvas = None
    mids, tops, bottoms = [], [], []
    for n, (lo, hi) in enumerate(zip(starts, ends)):
        above, below = halos[n]
        canvas, mid = layer(
            f"fine{n}", features, above, below, fine_codes, fine_weight, fine_bias, lo, hi - lo, True, canvas
        )
        mids.append(mid)
        tops.append(lax.ppermute(mid, "tile", up))
        bottoms.append(lax.ppermute(mid, "tile", down))
    coarse_in = jnp.concatenate(mids, axis=1)
    above = jnp.concatenate(tops, axis=1)
    below = jnp.concatenate(bottoms, axis=1)
    coarse_map, sums = layer(
        "coarse", coarse_in, above, below, coarse_codes, coarse_weight, coarse_bias, 0, coarse_in.shape[1] // USE, False
    )
    real_count = jnp.sum((coarse_links >> 8 & 1).astype(jnp.float32))
    totals, counted = lax.psum((jnp.sum(sums, axis=0), real_count), "tile")
    return (canvas, coarse_map, totals / counted)


def solution(mesh):
    return jax.shard_map(
        on_device,
        mesh=mesh,
        in_specs=(
            P(("parts", "tile"), None, None),
            P(("parts", "tile"), None),
            P(("parts", "tile"), None),
            P(),
            P(),
            P(),
            P(),
        ),
        out_specs=(P(("parts", "tile"), None, None), P(("parts", "tile"), None, None), P("parts")),
        check_vma=False,
    )
```

```python
import jax
import jax.numpy as jnp
import numpy as np
from jax import lax
from jax.experimental import pallas as pl
from jax.experimental.pallas import tpu as pltpu
from jax.sharding import PartitionSpec as P

USE = 64
WIN = 80
EDGE = 16
DEEP = 4
link_steps = ((-1, 0), (1, 0), (0, -1), (0, 1), (-1, -1), (-1, 1), (1, -1), (1, 1))


def bit_table():
    table = np.zeros((WIN, 256), np.int32)
    for bit, (dr, dc) in enumerate(link_steps):
        for i in range(WIN):
            table[i, (dr + 1) * WIN + (i + dc) % WIN] = 1 << bit
    return table


def pool_tables():
    first = np.zeros((64, 256), np.float32)
    for row in range(2):
        for col in range(32):
            for dr in range(2):
                for dc in range(2):
                    first[row * 32 + col, (2 * row + dr) * 64 + 2 * col + dc] = 0.25
    second = np.zeros((16, 64), np.float32)
    for col in range(16):
        for dr in range(2):
            for dc in range(2):
                second[col, dr * 32 + 2 * col + dc] = 0.25
    return first, second


def window_kernel(rows, pool, refs):
    (main, left, right, tmain, tleft, tright, bmain, bleft, bright, codes, outer, bits, w01, w23, w4, bias) = refs[:16]
    rest = refs[16:]
    if pool:
        pool1, pool2, _, out, coarse = rest[:5]
        rest = rest[5:]
    else:
        out, sums = rest[:2]
        rest = rest[2:]
    p0, p1, p2, p3, p4, links, coef = rest
    step = pl.program_id(0)
    full = rows + 2 * DEEP

    @pl.when(step == 0)
    def _():
        for ref in (p0, p1, p2, p3, p4):
            ref[...] = jnp.zeros_like(ref)
        if not pool:
            sums[...] = jnp.zeros_like(sums)

    def tables(code):
        degree = jnp.zeros(code.shape, jnp.int32)
        for bit in range(8):
            degree = degree + ((code >> bit) & 1)
        return code, -2.0 / jnp.maximum(degree.astype(jnp.float32), 1.0), ((code >> 8) & 1).astype(jnp.float32)

    inside, beyond = tables(codes[0]), tables(outer[0])

    def column(which, r):
        if r < DEEP:
            return beyond[which][:, r : r + 1]
        if r < DEEP + rows:
            return inside[which][:, r - DEEP : r - DEEP + 1]
        return beyond[which][:, r - rows : r - rows + 1]

    table = bits[...]
    low = lax.broadcasted_iota(jnp.int32, (EDGE, 128), 0) < 8

    for r in range(full):
        if r < DEEP:
            m, a, b, s = tmain, tleft, tright, r
        elif r < DEEP + rows:
            m, a, b, s = main, left, right, r - DEEP
        else:
            m, a, b, s = bmain, bleft, bright, r - DEEP - rows
        mask = jnp.broadcast_to(column(2, r), (WIN, 128))
        side = jnp.where(low, b[s].astype(jnp.float32), a[s].astype(jnp.float32))
        p0[pl.ds(r * WIN, USE), :] = (m[s].astype(jnp.float32) * mask[:USE]).astype(jnp.bfloat16)
        p0[pl.ds(r * WIN + USE, EDGE), :] = (side * mask[USE:]).astype(jnp.bfloat16)
        if 1 <= r < full - 1:
            wide = jnp.broadcast_to(column(0, r), (WIN, 256))
            links[r] = jnp.where((wide & table) != 0, 1.0, 0.0).astype(jnp.bfloat16)
            coef[r] = jnp.broadcast_to(column(1, r), (WIN, 128))

    terms = (p0, p1, p2, p3, p4)
    for k in range(1, 5):
        src, dst = terms[k - 1], terms[k]
        for r in range(k, full - k):
            acc = jnp.dot(links[r], src[pl.ds((r - 1) * WIN, 256), :], preferred_element_type=jnp.float32)
            if k == 1:
                fresh = acc * (0.5 * coef[r])
            else:
                fresh = acc * coef[r] - terms[k - 2][pl.ds(r * WIN, WIN), :].astype(jnp.float32)
            dst[pl.ds(r * WIN, WIN), :] = fresh.astype(jnp.bfloat16)

    def gather(ref, first, count):
        return jnp.concatenate([ref[pl.ds((first + j) * WIN, USE), :] for j in range(count)], axis=0)

    group = 4
    for g in range(rows // group):
        first = DEEP + g * group
        q = [gather(t, first, group) for t in terms]
        mixed = jnp.dot(jnp.concatenate([q[0], q[1]], axis=1), w01[...], preferred_element_type=jnp.float32)
        mixed += jnp.dot(jnp.concatenate([q[2], q[3]], axis=1), w23[...], preferred_element_type=jnp.float32)
        mixed += jnp.dot(q[4], w4[...], preferred_element_type=jnp.float32)
        mask = jnp.concatenate(
            [jnp.broadcast_to(column(2, first + j)[:USE], (USE, 128)) for j in range(group)], axis=0
        )
        res = (mask * jnp.maximum(mixed + bias[...], 0.0)).astype(jnp.bfloat16)
        for j in range(group):
            out[g * group + j] = res[j * USE : (j + 1) * USE]
        if pool:
            half = jnp.dot(pool1[...], res, preferred_element_type=jnp.float32).astype(jnp.bfloat16)
            coarse[g] = jnp.dot(pool2[...], half, preferred_element_type=jnp.float32).astype(jnp.bfloat16)
        else:
            sums[...] += jnp.sum(res.astype(jnp.float32).reshape(-1, 8, 128), axis=0)


def layer(name, main, top, bottom, origin, codes, outer, weights, bias, first, count, pool, canvas=None):
    rows, cols, width = main.shape
    total = cols // USE
    held = top.shape[1] // EDGE
    ratio = USE // EDGE

    def spec(n, pick, size):
        return pl.BlockSpec((n, size, width), lambda w: (0, pick(w), 0))

    def left_of(w):
        return jnp.maximum((first + w) * ratio - 1, 0)

    def right_of(w):
        return jnp.minimum((first + w) * ratio + ratio, total * ratio - 1)

    halo = [
        spec(DEEP, lambda w: first + w - origin, USE),
        spec(DEEP, lambda w: jnp.maximum((first + w - origin) * ratio - 1, 0), EDGE),
        spec(DEEP, lambda w: jnp.minimum((first + w - origin) * ratio + ratio, held - 1), EDGE),
    ]

    def whole(*shape):
        return pl.BlockSpec(shape, lambda w: (0,) * len(shape))

    full = rows + 2 * DEEP
    in_specs = (
        [spec(rows, lambda w: first + w, USE), spec(rows, left_of, EDGE), spec(rows, right_of, EDGE)]
        + halo + halo
        + [pl.BlockSpec((1, WIN, rows), lambda w: (first + w, 0, 0))]
        + [pl.BlockSpec((1, WIN, 2 * DEEP), lambda w: (first + w, 0, 0))]
        + [whole(WIN, 256), whole(256, 128), whole(256, 128), whole(128, 128), whole(1, 128)]
    )
    operands = [main] * 3 + [top] * 3 + [bottom] * 3 + [codes, outer, jnp.asarray(bit_table())]
    operands += [weights[0:2].reshape(256, 128), weights[2:4].reshape(256, 128), weights[4], bias.reshape(1, 128)]
    out_map = jax.ShapeDtypeStruct((rows, cols, width), jnp.bfloat16)
    aliases = {}
    if pool:
        pool1, pool2 = pool_tables()
        operands += [jnp.asarray(pool1, jnp.bfloat16), jnp.asarray(pool2, jnp.bfloat16)]
        in_specs += [whole(64, 256), whole(16, 64)]
        if canvas is None:
            operands.append(bias.reshape(1, 128))
            in_specs.append(whole(1, 128))
        else:
            aliases = {len(operands): 0}
            operands.append(canvas)
            in_specs.append(pl.BlockSpec(memory_space=pl.ANY))
        out_shape = [out_map, jax.ShapeDtypeStruct((rows // 4, count * USE // 4, width), jnp.bfloat16)]
        out_specs = [spec(rows, lambda w: first + w, USE), spec(rows // 4, lambda w: w, USE // 4)]
    else:
        out_shape = [out_map, jax.ShapeDtypeStruct((8, 128), jnp.float32)]
        out_specs = [spec(rows, lambda w: first + w, USE), whole(8, 128)]
    field = pltpu.VMEM((full * WIN + 16, 128), jnp.bfloat16)
    pixels = full * WIN * count
    return pl.pallas_call(
        lambda *refs: window_kernel(rows, pool, refs),
        grid=(count,),
        in_specs=in_specs,
        out_specs=out_specs,
        out_shape=out_shape,
        input_output_aliases=aliases,
        scratch_shapes=[field] * 5
        + [pltpu.VMEM((full, WIN, 256), jnp.bfloat16), pltpu.VMEM((full, WIN, 128), jnp.float32)],
        compiler_params=pltpu.CompilerParams(vmem_limit_bytes=40 * 2**20),
        cost_estimate=pl.CostEstimate(
            flops=pixels * 128 * 2 * 256 * 4, bytes_accessed=pixels * 128 * 4, transcendentals=0
        ),
        name=name,
    )(*operands)


def shifts():
    size = lax.axis_size("tile")
    up = [(i, i + 1) for i in range(size - 1)]
    down = [(i + 1, i) for i in range(size - 1)]
    return up, down


def code_windows(codes):
    rows, cols = codes.shape
    count = cols // USE
    body = codes.reshape(rows, count, USE)
    after = jnp.pad(codes[:, USE:], ((0, 0), (0, USE))).reshape(rows, count, USE)[:, :, :8]
    before = jnp.pad(codes[:, :-USE], ((0, 0), (USE, 0))).reshape(rows, count, USE)[:, :, USE - 8 :]
    return jnp.concatenate([body, after, before], axis=2).transpose(1, 2, 0)


def coded(codes):
    return jnp.stack([codes & 255, codes >> 8]).astype(jnp.bfloat16).reshape(-1, 128)


def decoded(lines, shape):
    pair = lines.reshape((2,) + shape).astype(jnp.int32)
    return pair[0] + 256 * pair[1]


def total_kernel(size, part, pooled, slots, send_sem, recv_sem):
    me = lax.axis_index("tile")
    barrier = pltpu.get_barrier_semaphore()
    for hop in range(1, size):
        pl.semaphore_signal(
            barrier, inc=1, device_id={"tile": lax.rem(me + hop, size)}, device_id_type=pl.DeviceIdType.MESH
        )
    pl.semaphore_wait(barrier, size - 1)

    def copy(hop):
        return pltpu.make_async_remote_copy(
            src_ref=part,
            dst_ref=slots.at[me],
            send_sem=send_sem.at[hop],
            recv_sem=recv_sem.at[hop],
            device_id={"tile": lax.rem(me + hop, size)},
            device_id_type=pl.DeviceIdType.MESH,
        )

    copies = [copy(hop) for hop in range(1, size)]
    for one in copies:
        one.start()
    slots[me] = part[...]
    for hop in range(1, size):
        sender = lax.rem(me + size - hop, size)
        pltpu.make_async_remote_copy(
            src_ref=part,
            dst_ref=slots.at[sender],
            send_sem=send_sem.at[hop],
            recv_sem=recv_sem.at[hop],
            device_id={"tile": lax.rem(me + hop, size)},
            device_id_type=pl.DeviceIdType.MESH,
        ).wait()
    whole = slots[0]
    for j in range(1, size):
        whole = whole + slots[j]
    pooled[...] = jnp.sum(whole[:8], axis=0, keepdims=True) / whole[8:9]


def total_over_tiles(part):
    size = lax.axis_size("tile")
    return pl.pallas_call(
        lambda *refs: total_kernel(size, *refs),
        in_specs=[pl.BlockSpec(memory_space=pltpu.VMEM)],
        out_specs=pl.BlockSpec(memory_space=pltpu.VMEM),
        out_shape=jax.ShapeDtypeStruct((1, 128), jnp.float32),
        scratch_shapes=[
            pltpu.VMEM((size, 16, 128), jnp.float32),
            pltpu.SemaphoreType.DMA((size,)),
            pltpu.SemaphoreType.DMA((size,)),
        ],
        compiler_params=pltpu.CompilerParams(collective_id=0, has_side_effects=True),
        name="total",
    )(part)


SPLITS = (0.3, 0.9, 1.0)


def on_device(features, links, coarse_links, fine_weight, fine_bias, coarse_weight, coarse_bias):
    up, down = shifts()
    rows, cols, width = features.shape
    total = cols // USE
    ends = [round(total * f) for f in SPLITS]
    starts = [0] + ends[:-1]
    split = ends[0] * USE
    near = (DEEP, split + USE, width)
    lines = near[0] * near[1]
    fine_lines = DEEP * cols * 2 // 128

    def exchanged(pick, coarse_pick):
        return jnp.concatenate(
            [features[pick, : split + USE].reshape(-1, 128), coded(links[pick]), coded(coarse_links[coarse_pick])]
        )

    last, start = slice(rows - DEEP, rows), slice(0, DEEP)
    coarse_rows = coarse_links.shape[0]
    above = lax.ppermute(exchanged(last, slice(coarse_rows - DEEP, coarse_rows)), "tile", up)
    below = lax.ppermute(exchanged(start, start), "tile", down)
    far_above = lax.ppermute(features[last, split - USE :], "tile", up)
    far_below = lax.ppermute(features[start, split - USE :], "tile", down)
    fine_codes = code_windows(links)
    coarse_codes = code_windows(coarse_links)
    ghosts = [decoded(part[lines : lines + fine_lines], (DEEP, cols)) for part in (above, below)]
    fine_outer = code_windows(jnp.concatenate(ghosts))
    ghosts = [decoded(part[lines + fine_lines :], (DEEP, cols // 4)) for part in (above, below)]
    coarse_outer = code_windows(jnp.concatenate(ghosts))
    halos = [(above[:lines].reshape(near), below[:lines].reshape(near), 0)]
    halos += [(far_above, far_below, ends[0] - 1)] * (len(ends) - 1)
    canvas = None
    mids, tops, bottoms = [], [], []
    for n, (lo, hi) in enumerate(zip(starts, ends)):
        canvas, mid = layer(
            f"fine{n}", features, *halos[n], fine_codes, fine_outer, fine_weight, fine_bias, lo, hi - lo, True, canvas
        )
        mids.append(mid)
        if n == 0:
            continue
        send = jnp.concatenate(mids[:2], axis=1) if n == 1 else mid
        tops.append(lax.ppermute(send, "tile", up))
        bottoms.append(lax.ppermute(send, "tile", down))
    coarse_in = jnp.concatenate(mids, axis=1)
    coarse_map, sums = layer(
        "coarse", coarse_in, jnp.concatenate(tops, axis=1), jnp.concatenate(bottoms, axis=1), 0,
        coarse_codes, coarse_outer, coarse_weight, coarse_bias, 0, coarse_in.shape[1] // USE, False,
    )
    real_count = jnp.sum((coarse_links >> 8 & 1).astype(jnp.float32))
    pooled = total_over_tiles(jnp.concatenate([sums, jnp.broadcast_to(real_count, (8, 128))]))
    return (canvas, coarse_map, pooled[0])


def solution(mesh):
    return jax.shard_map(
        on_device,
        mesh=mesh,
        in_specs=(
            P(("parts", "tile"), None, None),
            P(("parts", "tile"), None),
            P(("parts", "tile"), None),
            P(),
            P(),
            P(),
            P(),
        ),
        out_specs=(P(("parts", "tile"), None, None), P(("parts", "tile"), None, None), P("parts")),
        check_vma=False,
    )
```

```python
import jax
import jax.numpy as jnp
import numpy as np
from jax import lax
from jax.experimental import pallas as pl
from jax.experimental.pallas import tpu as pltpu
from jax.sharding import PartitionSpec as P

USE = 64
WIN = 80
EDGE = 16
DEEP = 4
link_steps = ((-1, 0), (1, 0), (0, -1), (0, 1), (-1, -1), (-1, 1), (1, -1), (1, 1))


def bit_table():
    table = np.zeros((WIN, 256), np.int32)
    for bit, (dr, dc) in enumerate(link_steps):
        for i in range(WIN):
            table[i, (dr + 1) * WIN + (i + dc) % WIN] = 1 << bit
    return table


def pool_tables():
    first = np.zeros((64, 256), np.float32)
    for row in range(2):
        for col in range(32):
            for dr in range(2):
                for dc in range(2):
                    first[row * 32 + col, (2 * row + dr) * 64 + 2 * col + dc] = 0.25
    second = np.zeros((16, 64), np.float32)
    for col in range(16):
        for dr in range(2):
            for dc in range(2):
                second[col, dr * 32 + 2 * col + dc] = 0.25
    return first, second


def window_kernel(rows, pool, refs):
    (main, left, right, tmain, tleft, tright, bmain, bleft, bright, codes, outer, bits, w01, w23, w4, bias) = refs[:16]
    rest = refs[16:]
    if pool:
        pool1, pool2, _, out, coarse = rest[:5]
        rest = rest[5:]
    else:
        out, sums = rest[:2]
        rest = rest[2:]
    p0, p1, p2, p3, p4, links, coef = rest
    step = pl.program_id(0)
    full = rows + 2 * DEEP

    @pl.when(step == 0)
    def _():
        for ref in (p0, p1, p2, p3, p4):
            ref[...] = jnp.zeros_like(ref)
        if not pool:
            sums[...] = jnp.zeros_like(sums)

    def tables(code):
        degree = jnp.zeros(code.shape, jnp.int32)
        for bit in range(8):
            degree = degree + ((code >> bit) & 1)
        return code, -2.0 / jnp.maximum(degree.astype(jnp.float32), 1.0), ((code >> 8) & 1).astype(jnp.float32)

    inside, beyond = tables(codes[0]), tables(outer[0])

    def column(which, r):
        if r < DEEP:
            return beyond[which][:, r : r + 1]
        if r < DEEP + rows:
            return inside[which][:, r - DEEP : r - DEEP + 1]
        return beyond[which][:, r - rows : r - rows + 1]

    table = bits[...]
    low = lax.broadcasted_iota(jnp.int32, (EDGE, 128), 0) < 8

    for r in range(full):
        if r < DEEP:
            m, a, b, s = tmain, tleft, tright, r
        elif r < DEEP + rows:
            m, a, b, s = main, left, right, r - DEEP
        else:
            m, a, b, s = bmain, bleft, bright, r - DEEP - rows
        mask = jnp.broadcast_to(column(2, r), (WIN, 128))
        side = jnp.where(low, b[s].astype(jnp.float32), a[s].astype(jnp.float32))
        p0[pl.ds(r * WIN, USE), :] = (m[s].astype(jnp.float32) * mask[:USE]).astype(jnp.bfloat16)
        p0[pl.ds(r * WIN + USE, EDGE), :] = (side * mask[USE:]).astype(jnp.bfloat16)
        if 1 <= r < full - 1:
            wide = jnp.broadcast_to(column(0, r), (WIN, 256))
            links[r] = jnp.where((wide & table) != 0, 1.0, 0.0).astype(jnp.bfloat16)
            coef[r] = jnp.broadcast_to(column(1, r), (WIN, 128))

    terms = (p0, p1, p2, p3, p4)
    for k in range(1, 5):
        src, dst = terms[k - 1], terms[k]
        for r in range(k, full - k):
            acc = jnp.dot(links[r], src[pl.ds((r - 1) * WIN, 256), :], preferred_element_type=jnp.float32)
            if k == 1:
                fresh = acc * (0.5 * coef[r])
            else:
                fresh = acc * coef[r] - terms[k - 2][pl.ds(r * WIN, WIN), :].astype(jnp.float32)
            dst[pl.ds(r * WIN, WIN), :] = fresh.astype(jnp.bfloat16)

    def gather(ref, first, count):
        return jnp.concatenate([ref[pl.ds((first + j) * WIN, USE), :] for j in range(count)], axis=0)

    group = 4
    for g in range(rows // group):
        first = DEEP + g * group
        q = [gather(t, first, group) for t in terms]
        mixed = jnp.dot(jnp.concatenate([q[0], q[1]], axis=1), w01[...], preferred_element_type=jnp.float32)
        mixed += jnp.dot(jnp.concatenate([q[2], q[3]], axis=1), w23[...], preferred_element_type=jnp.float32)
        mixed += jnp.dot(q[4], w4[...], preferred_element_type=jnp.float32)
        mask = jnp.concatenate(
            [jnp.broadcast_to(column(2, first + j)[:USE], (USE, 128)) for j in range(group)], axis=0
        )
        res = (mask * jnp.maximum(mixed + bias[...], 0.0)).astype(jnp.bfloat16)
        for j in range(group):
            out[g * group + j] = res[j * USE : (j + 1) * USE]
        if pool:
            half = jnp.dot(pool1[...], res, preferred_element_type=jnp.float32).astype(jnp.bfloat16)
            coarse[g] = jnp.dot(pool2[...], half, preferred_element_type=jnp.float32).astype(jnp.bfloat16)
        else:
            sums[...] += jnp.sum(res.astype(jnp.float32).reshape(-1, 8, 128), axis=0)


def layer(name, main, top, bottom, origin, codes, outer, skip, weights, bias, first, count, pool, canvas=None):
    rows, cols, width = main.shape
    total = cols // USE
    held = top.shape[1] // EDGE
    ratio = USE // EDGE

    def spec(n, pick, size):
        return pl.BlockSpec((n, size, width), lambda w: (0, pick(w), 0))

    def left_of(w):
        return jnp.maximum((first + w) * ratio - 1, 0)

    def right_of(w):
        return jnp.minimum((first + w) * ratio + ratio, total * ratio - 1)

    halo = [
        spec(DEEP, lambda w: first + w - origin, USE),
        spec(DEEP, lambda w: jnp.maximum((first + w - origin) * ratio - 1, 0), EDGE),
        spec(DEEP, lambda w: jnp.minimum((first + w - origin) * ratio + ratio, held - 1), EDGE),
    ]

    def whole(*shape):
        return pl.BlockSpec(shape, lambda w: (0,) * len(shape))

    full = rows + 2 * DEEP
    in_specs = (
        [spec(rows, lambda w: first + w, USE), spec(rows, left_of, EDGE), spec(rows, right_of, EDGE)]
        + halo + halo
        + [pl.BlockSpec((1, WIN, rows), lambda w: (first + w, 0, 0))]
        + [pl.BlockSpec((1, WIN, 2 * DEEP), lambda w: (skip + first + w, 0, 0))]
        + [whole(WIN, 256), whole(256, 128), whole(256, 128), whole(128, 128), whole(1, 128)]
    )
    operands = [main] * 3 + [top] * 3 + [bottom] * 3 + [codes, outer, jnp.asarray(bit_table())]
    operands += [weights[0:2].reshape(256, 128), weights[2:4].reshape(256, 128), weights[4], bias.reshape(1, 128)]
    out_map = jax.ShapeDtypeStruct((rows, cols, width), jnp.bfloat16)
    aliases = {}
    if pool:
        pool1, pool2 = pool_tables()
        operands += [jnp.asarray(pool1, jnp.bfloat16), jnp.asarray(pool2, jnp.bfloat16)]
        in_specs += [whole(64, 256), whole(16, 64)]
        if canvas is None:
            operands.append(bias.reshape(1, 128))
            in_specs.append(whole(1, 128))
        else:
            aliases = {len(operands): 0}
            operands.append(canvas)
            in_specs.append(pl.BlockSpec(memory_space=pl.ANY))
        out_shape = [out_map, jax.ShapeDtypeStruct((rows // 4, count * USE // 4, width), jnp.bfloat16)]
        out_specs = [spec(rows, lambda w: first + w, USE), spec(rows // 4, lambda w: w, USE // 4)]
    else:
        out_shape = [out_map, jax.ShapeDtypeStruct((8, 128), jnp.float32)]
        out_specs = [spec(rows, lambda w: first + w, USE), whole(8, 128)]
    field = pltpu.VMEM((full * WIN + 16, 128), jnp.bfloat16)
    pixels = full * WIN * count
    return pl.pallas_call(
        lambda *refs: window_kernel(rows, pool, refs),
        grid=(count,),
        in_specs=in_specs,
        out_specs=out_specs,
        out_shape=out_shape,
        input_output_aliases=aliases,
        scratch_shapes=[field] * 5
        + [pltpu.VMEM((full, WIN, 256), jnp.bfloat16), pltpu.VMEM((full, WIN, 128), jnp.float32)],
        compiler_params=pltpu.CompilerParams(vmem_limit_bytes=40 * 2**20),
        cost_estimate=pl.CostEstimate(
            flops=pixels * 128 * 2 * 256 * 4, bytes_accessed=pixels * 128 * 4, transcendentals=0
        ),
        name=name,
    )(*operands)


def shifts():
    size = lax.axis_size("tile")
    up = [(i, i + 1) for i in range(size - 1)]
    down = [(i + 1, i) for i in range(size - 1)]
    return up, down


def code_windows(codes):
    rows, cols = codes.shape
    count = cols // USE
    body = codes.reshape(rows, count, USE)
    after = jnp.pad(codes[:, USE:], ((0, 0), (0, USE))).reshape(rows, count, USE)[:, :, :8]
    before = jnp.pad(codes[:, :-USE], ((0, 0), (USE, 0))).reshape(rows, count, USE)[:, :, USE - 8 :]
    return jnp.concatenate([body, after, before], axis=2).transpose(1, 2, 0)


def coded(codes):
    return jnp.stack([codes & 255, codes >> 8]).astype(jnp.bfloat16).reshape(-1, 128)


def decoded(lines, shape):
    pair = lines.reshape((2,) + shape).astype(jnp.int32)
    return pair[0] + 256 * pair[1]


def total_kernel(size, part, pooled, slots, send_sem, recv_sem):
    me = lax.axis_index("tile")
    barrier = pltpu.get_barrier_semaphore()
    for hop in range(1, size):
        pl.semaphore_signal(
            barrier, inc=1, device_id={"tile": lax.rem(me + hop, size)}, device_id_type=pl.DeviceIdType.MESH
        )
    pl.semaphore_wait(barrier, size - 1)

    def copy(hop):
        return pltpu.make_async_remote_copy(
            src_ref=part,
            dst_ref=slots.at[me],
            send_sem=send_sem.at[hop],
            recv_sem=recv_sem.at[hop],
            device_id={"tile": lax.rem(me + hop, size)},
            device_id_type=pl.DeviceIdType.MESH,
        )

    copies = [copy(hop) for hop in range(1, size)]
    for one in copies:
        one.start()
    slots[me] = part[...]
    for hop in range(1, size):
        sender = lax.rem(me + size - hop, size)
        pltpu.make_async_remote_copy(
            src_ref=part,
            dst_ref=slots.at[sender],
            send_sem=send_sem.at[hop],
            recv_sem=recv_sem.at[hop],
            device_id={"tile": lax.rem(me + hop, size)},
            device_id_type=pl.DeviceIdType.MESH,
        ).wait()
    whole = slots[0]
    for j in range(1, size):
        whole = whole + slots[j]
    pooled[...] = jnp.sum(whole[:8], axis=0, keepdims=True) / whole[8:9]


def total_over_tiles(part):
    size = lax.axis_size("tile")
    return pl.pallas_call(
        lambda *refs: total_kernel(size, *refs),
        in_specs=[pl.BlockSpec(memory_space=pltpu.VMEM)],
        out_specs=pl.BlockSpec(memory_space=pltpu.VMEM),
        out_shape=jax.ShapeDtypeStruct((1, 128), jnp.float32),
        scratch_shapes=[
            pltpu.VMEM((size, 16, 128), jnp.float32),
            pltpu.SemaphoreType.DMA((size,)),
            pltpu.SemaphoreType.DMA((size,)),
        ],
        compiler_params=pltpu.CompilerParams(collective_id=0, has_side_effects=True),
        name="total",
    )(part)


SPLITS = (0.15, 0.45, 0.92, 1.0)


def on_device(features, links, coarse_links, fine_weight, fine_bias, coarse_weight, coarse_bias):
    up, down = shifts()
    rows, cols, width = features.shape
    total = cols // USE
    ends = [round(total * f) for f in SPLITS]
    starts = [0] + ends[:-1]
    near = (DEEP, (ends[0] + 1) * USE, width)
    lines = near[0] * near[1]
    all_cols = cols + coarse_links.shape[1]

    def exchanged(pick, coarse_pick):
        codes = jnp.concatenate([links[pick], coarse_links[coarse_pick]], axis=1)
        return jnp.concatenate([features[pick, : near[1]].reshape(-1, 128), coded(codes)])

    last, start = slice(rows - DEEP, rows), slice(0, DEEP)
    coarse_rows = coarse_links.shape[0]
    above = lax.ppermute(exchanged(last, slice(coarse_rows - DEEP, coarse_rows)), "tile", up)
    below = lax.ppermute(exchanged(start, start), "tile", down)
    halos = [(above[:lines].reshape(near), below[:lines].reshape(near), 0)]

    def further(lo, hi, after):
        pair = (features[last, lo * USE : hi * USE], features[start, lo * USE : hi * USE])
        pair, _ = lax.optimization_barrier((pair, after))
        return lax.ppermute(pair[0], "tile", up), lax.ppermute(pair[1], "tile", down), lo

    halos.append(further(ends[0] - 1, ends[1] + 1, (above, below)))
    fine_codes, coarse_codes = lax.optimization_barrier((code_windows(links), code_windows(coarse_links)))
    ghosts = [decoded(part[lines:], (DEEP, all_cols)) for part in (above, below)]
    outer = code_windows(jnp.concatenate(ghosts))
    canvas = None
    mids, tops, bottoms = [], [], []
    for n, (lo, hi) in enumerate(zip(starts, ends)):
        canvas, mid = layer(
            f"fine{n}", features, *halos[n], fine_codes, outer, 0, fine_weight, fine_bias, lo, hi - lo, True, canvas
        )
        mids.append(mid)
        if n == 0:
            halos += [further(ends[1] - 1, total, (mid, halos[1][0], halos[1][1]))] * 2
        if n < 2:
            continue
        send = jnp.concatenate(mids, axis=1) if n == 2 else mid
        tops.append(lax.ppermute(send, "tile", up))
        bottoms.append(lax.ppermute(send, "tile", down))
    coarse_in = jnp.concatenate(mids, axis=1)
    coarse_map, sums = layer(
        "coarse", coarse_in, jnp.concatenate(tops, axis=1), jnp.concatenate(bottoms, axis=1), 0,
        coarse_codes, outer, total, coarse_weight, coarse_bias, 0, coarse_in.shape[1] // USE, False,
    )
    real_count = jnp.sum((coarse_links >> 8 & 1).astype(jnp.float32))
    pooled = total_over_tiles(jnp.concatenate([sums, jnp.broadcast_to(real_count, (8, 128))]))
    return (canvas, coarse_map, pooled[0])


def solution(mesh):
    return jax.shard_map(
        on_device,
        mesh=mesh,
        in_specs=(
            P(("parts", "tile"), None, None),
            P(("parts", "tile"), None),
            P(("parts", "tile"), None),
            P(),
            P(),
            P(),
            P(),
        ),
        out_specs=(P(("parts", "tile"), None, None), P(("parts", "tile"), None, None), P("parts")),
        check_vma=False,
    )
```
